32 devices in a mesh: ens: 2 (over x), lon: 16 (over z, y, core).
Axes of the slice: x: 2, y: 2, z: 4, core: 2. Of those that a mesh axis runs over, the one named last changes fastest.
Arguments:
- activations: bfloat16 [128, 768, 256], P('ens', 'lon'), parts along dimension 0, may hold values from -6 to 6
- quadrature: bfloat16 [4, 64, 3, 16], replicated, may hold values from -1.5 to 1.5
- support: int32 [4, 16], replicated, may hold values from -24 to 24, as said below
- support_count: int32 [4], replicated, may hold values from 2 to 16, as said below
- weight_first: bfloat16 [4, 256, 256], replicated, may hold values from -0.1875 to 0.1875
- weight_second: bfloat16 [4, 256, 256], replicated, may hold values from -0.1875 to 0.1875
- cotangent: bfloat16 [128, 768, 256], P('ens', 'lon'), parts along dimension 0, may hold values from -6 to 6
Outputs:
- mixed: bfloat16 [128, 768, 256], P('ens', 'lon'), parts along dimension 0
- grad_field: bfloat16 [128, 768, 256], P('ens', 'lon'), parts along dimension 0
- grad_first: float32 [8, 256, 256], P('ens'), parts along dimension 0
- grad_second: float32 [8, 256, 256], P('ens'), parts along dimension 0
The draws below stay inside these ranges and needn't reach their ends.
There are 2 independent parts, one for each index of `ens`. The reference program is written for one: setup_inputs(seed, part) draws one part's arguments, and reference() takes and returns one part's arrays. A program takes and returns all parts, laid end to end along the dimension named above; an argument that names none is the same for every part. Nothing has to cross between parts.
Inputs may be any that keep to these rules, and one draw needn't show every extreme that they name: In band b the first support_count[b] entries of support[b] are distinct, lie within -reach(b) .. reach(b), and include both -reach(b) and reach(b); the remaining entries are padding. `support_count`: for band b at most min(16, 2 reach(b) + 1); the last band's count is 16.
All inputs are finite; a program needn't handle non-finite values.
Results may differ from the reference program's by a relative error of at most 0.015.
Values may be sent and summed in bfloat16 or wider, within the bound.
A program may use at most 192 MiB of HBM per device.

```python
import jax
import jax.numpy as jnp
from jax import lax

C = 256
K = 4
S = 16
BAND_ROWS = 16
NB = 4
HMAX = 24
NLAT = 64
NLON = 768


def support_tables(key):
    offset_list = []
    length_list = []
    for band_id in range(NB):
        reach_cols = HMAX * (band_id + 1) // NB
        option_count = 2 * reach_cols + 1
        capacity = min(S, option_count)
        band_key = jax.random.fold_in(key, band_id)
        key_length, key_perm, key_fill, key_order = jax.random.split(band_key, 4)
        if band_id == NB - 1:
            length_now = jnp.int32(capacity)
        else:
            length_now = jax.random.randint(key_length, (), 2, capacity + 1, dtype=jnp.int32)
        shuffled = jax.random.permutation(key_perm, option_count).astype(jnp.int32)
        position = jnp.arange(option_count, dtype=jnp.int32)
        ranking = jnp.where(shuffled == 0, -2, jnp.where(shuffled == option_count - 1, -1, position))
        ordered = shuffled[jnp.argsort(ranking, stable=True)]
        if option_count >= S:
            chosen = ordered[:S]
        else:
            chosen = jnp.concatenate([ordered, jnp.zeros((S - option_count,), jnp.int32) + reach_cols])
        slot_pos = jnp.arange(S, dtype=jnp.int32)
        live_mask = slot_pos < length_now
        filler = jax.random.randint(key_fill, (S,), -HMAX, HMAX + 1, dtype=jnp.int32)
        row_now = jnp.where(live_mask, chosen - reach_cols, filler)
        noise = jax.random.randint(key_order, (S,), 0, 1024, dtype=jnp.int32)
        ranks = jnp.where(live_mask, noise * S + slot_pos, 1024 * S + slot_pos)
        offset_list.append(row_now[jnp.argsort(ranks, stable=True)])
        length_list.append(length_now)
    return (jnp.stack(offset_list), jnp.stack(length_list).astype(jnp.int32))


def draw_support(key, part):
    tables = support_tables(key)
    return tables[0]


def draw_support_count(key, part):
    tables = support_tables(key)
    return tables[1]


def levels(own_key, shape, shards, least, largest):
    def one(dim, blocks):
        steps = jax.random.uniform(jax.random.fold_in(jax.random.fold_in(own_key, 6), dim), (blocks,), jnp.float32, least / len(shards), largest / len(shards))
        return jnp.repeat(jnp.exp(steps), shape[dim] // blocks).reshape((-1,) + (1,) * (len(shape) - dim - 1))

    gain = one(*shards[0])
    for cut in shards[1:]:
        gain = gain * one(*cut)
    return gain


def gaussian(stream_key, dims, deviation, limit, cuts=(), held_as=jnp.bfloat16):
    values = deviation * jax.random.normal(stream_key, dims, jnp.float32)
    if cuts:
        values = values * levels(stream_key, dims, cuts, -0.22, 0.18)
    return jnp.clip(values, -limit, limit).astype(held_as)


def setup_inputs(seed: int = 0, part: int = 0) -> dict:
    arg_keys = jax.random.split(jax.random.key(seed), 8)
    part_splits = jax.random.split(jax.random.fold_in(arg_keys[7], part), 8)
    activations = gaussian(part_splits[0], (NLAT, NLON, C), 1.0, 6.0, ((1, 16),))
    quadrature = gaussian(arg_keys[1], (K, NLAT, 3, S), S ** -0.5, 1.5)
    support = draw_support(jax.random.fold_in(arg_keys[7], 71), part)
    support_count = draw_support_count(jax.random.fold_in(arg_keys[7], 71), part)
    weight_first = gaussian(arg_keys[4], (K, C, C), (K * C) ** -0.5, 0.1875)
    weight_second = gaussian(arg_keys[5], (K, C, C), (K * C) ** -0.5, 0.1875)
    cotangent = gaussian(part_splits[6], (NLAT, NLON, C), 1.0, 6.0, ((1, 16),))
    return {"activations": activations, "quadrature": quadrature, "support": support, "support_count": support_count, "weight_first": weight_first, "weight_second": weight_second, "cotangent": cotangent}


def gelu_value(value):
    return value * (0.5 + 0.5 * lax.erf(value * 0.7071067811865476))


def gelu_slope(value):
    density = jnp.exp(-0.5 * value * value) * 0.3989422804014327
    return 0.5 + 0.5 * lax.erf(value * 0.7071067811865476) + value * density


def spatial_map(field, quadrature, support, support_count):
    padded = jnp.pad(field.astype(jnp.float32), ((1, 1), (0, 0), (0, 0)))
    columns = jnp.arange(NLON, dtype=jnp.int32)
    kernel = quadrature.astype(jnp.float32)
    slot_ids = jnp.arange(S, dtype=jnp.int32)
    blocks = []
    for band_id in range(NB):
        first_row = band_id * BAND_ROWS
        rows_in = padded[first_row:first_row + BAND_ROWS + 2]
        band_kernel = kernel[:, first_row:first_row + BAND_ROWS]
        offsets = support[band_id]
        count_now = support_count[band_id]

        def add_slot(running, slot_index, rows_in=rows_in, band_kernel=band_kernel, offsets=offsets, count_now=count_now):
            live_mask = (slot_index < count_now).astype(jnp.float32)
            column_index = (columns + offsets[slot_index]) % NLON
            shifted = jnp.take(rows_in, column_index, axis=1)
            stacked = jnp.stack([shifted[lat_tap:lat_tap + BAND_ROWS] for lat_tap in range(3)], 1)
            weights_now = jnp.take(band_kernel, slot_index, axis=3) * live_mask
            update = jnp.einsum("kid,idjc->ijkc", weights_now, stacked, precision=lax.Precision.HIGHEST)
            return running + update, None

        start_value = jnp.zeros((BAND_ROWS, NLON, K, C), jnp.float32)
        blocks.append(lax.scan(add_slot, start_value, slot_ids)[0])
    return jnp.concatenate(blocks, 0).astype(jnp.bfloat16)


def adjoint_map(back, quadrature, support, support_count):
    source_all = back.astype(jnp.float32)
    columns = jnp.arange(NLON, dtype=jnp.int32)
    kernel = quadrature.astype(jnp.float32)
    slot_ids = jnp.arange(S, dtype=jnp.int32)
    result = jnp.zeros((NLAT + 2, NLON, C), jnp.float32)
    for band_id in range(NB):
        first_row = band_id * BAND_ROWS
        source = source_all[first_row:first_row + BAND_ROWS]
        band_kernel = kernel[:, first_row:first_row + BAND_ROWS]
        offsets = support[band_id]
        count_now = support_count[band_id]

        def add_slot(running, slot_index, source=source, band_kernel=band_kernel, offsets=offsets, count_now=count_now):
            live_mask = (slot_index < count_now).astype(jnp.float32)
            column_index = (columns - offsets[slot_index]) % NLON
            shifted = jnp.take(source, column_index, axis=1)
            weights_now = jnp.take(band_kernel, slot_index, axis=3) * live_mask
            spread = jnp.einsum("kid,ijkc->idjc", weights_now, shifted, precision=lax.Precision.HIGHEST)
            for lat_tap in range(3):
                running = running.at[lat_tap:lat_tap + BAND_ROWS].add(spread[:, lat_tap])
            return running, None

        start_value = jnp.zeros((BAND_ROWS + 2, NLON, C), jnp.float32)
        partial_value = lax.scan(add_slot, start_value, slot_ids)[0]
        result = result.at[first_row:first_row + BAND_ROWS + 2].add(partial_value)
    return result[1:-1]


def reference(activations, quadrature, support, support_count, weight_first, weight_second, cotangent):
    flat_first = weight_first.reshape(K * C, C)
    flat_second = weight_second.reshape(K * C, C)
    cells = NLAT * NLON
    grad_scale = 1.0 / (cells ** 0.5)
    spread_one = spatial_map(activations, quadrature, support, support_count).reshape(cells, K * C)
    preact = jnp.dot(spread_one, flat_first, preferred_element_type=jnp.float32)
    activated = gelu_value(preact).astype(jnp.bfloat16).reshape(NLAT, NLON, C)
    spread_two = spatial_map(activated, quadrature, support, support_count).reshape(cells, K * C)
    branch = jnp.dot(spread_two, flat_second, preferred_element_type=jnp.float32)
    mixed = (activations.reshape(cells, C).astype(jnp.float32) + branch).astype(jnp.bfloat16)
    cot_flat = cotangent.reshape(cells, C)
    grad_second = jnp.dot(spread_two.T, cot_flat, preferred_element_type=jnp.float32) * grad_scale
    back_two = jnp.dot(cot_flat, flat_second.T, preferred_element_type=jnp.float32).astype(jnp.bfloat16)
    grad_act = adjoint_map(back_two.reshape(NLAT, NLON, K, C), quadrature, support, support_count).reshape(cells, C)
    grad_pre = (grad_act * gelu_slope(preact)).astype(jnp.bfloat16)
    grad_first = jnp.dot(spread_one.T, grad_pre, preferred_element_type=jnp.float32) * grad_scale
    back_one = jnp.dot(grad_pre, flat_first.T, preferred_element_type=jnp.float32).astype(jnp.bfloat16)
    adjoint_one = adjoint_map(back_one.reshape(NLAT, NLON, K, C), quadrature, support, support_count)
    grad_field = (cotangent.astype(jnp.float32) + adjoint_one).astype(jnp.bfloat16)
    return (mixed.reshape(NLAT, NLON, C), grad_field, grad_first.reshape(K, C, C), grad_second.reshape(K, C, C))
```

```python
import functools
import math

import jax
import jax.numpy as jnp
from jax import lax
from jax.experimental import pallas as pl
from jax.experimental.pallas import tpu as pltpu
from jax.sharding import PartitionSpec as P

LANES = 128
VMEM_LIMIT = 56 * 1024 * 1024


def gelu_cdf(value):
    return 0.5 + 0.5 * lax.erf(value * 0.7071067811865476)


def gelu_slope(value):
    density = jnp.exp(-0.5 * value * value) * 0.3989422804014327
    return gelu_cdf(value) + value * density


def tap_tables(quadrature, support, support_count, halo):
    kernel_count, rows, taps, slots = quadrature.shape
    bands = support.shape[0]
    band_rows = rows // bands
    live = lax.broadcasted_iota(jnp.int32, support.shape, 1) < support_count[:, None]
    lane = jnp.arange(LANES, dtype=jnp.int32)
    by_band = quadrature.reshape(kernel_count, bands, band_rows, taps, slots)

    def place(sign):
        hot = ((halo + sign * support)[:, :, None] == lane) & live[:, :, None]
        table = jnp.einsum(
            "kbrds,bsl->brkdl", by_band, hot.astype(jnp.bfloat16), preferred_element_type=jnp.float32
        )
        return table.reshape(rows, kernel_count, taps, LANES)

    row = jnp.arange(rows)[:, None, None, None]
    tap = jnp.arange(taps)[None, None, :, None]
    inside = (row + tap >= 1) & (row + tap <= rows)
    ahead = jnp.where(inside, place(1), 0.0)
    source = jnp.pad(place(-1), ((1, 1), (0, 0), (0, 0), (0, 0)))
    back = jnp.stack([source[e : e + rows, :, taps - 1 - e] for e in range(taps)], 2)
    shape = (rows, kernel_count * taps, LANES)
    return ahead.reshape(shape), back.reshape(shape)


def fill_matrices(table_ref, matrix_ref, row, cols):
    table = table_ref[row]
    for k in range(table.shape[0] // 3):
        for d in range(3):
            line = jnp.broadcast_to(table[k * 3 + d][None], (cols, LANES))
            rolled = pltpu.roll(line, 0, 1, stride=1, stride_axis=0)
            matrix_ref[row, k * cols : (k + 1) * cols, d * LANES : (d + 1) * LANES] = rolled.astype(
                jnp.bfloat16
            )


def spread_block(own, low, high, matrix, matrix_row, spread, first_row, count):
    rows, cols, channels = own.shape
    filler = jnp.zeros((LANES - cols - 2 * low.shape[1], channels), jnp.bfloat16)
    for r in range(count):
        parts = []
        for d in range(3):
            src = jnp.clip(first_row + r + d - 1, 0, rows - 1)
            parts += [low[src], own[src], high[src], filler]
        mixed = jnp.dot(
            matrix[matrix_row + r],
            jnp.concatenate(parts, 0),
            preferred_element_type=jnp.float32,
        ).astype(jnp.bfloat16)
        for k in range(mixed.shape[0] // cols):
            spread[r * cols : (r + 1) * cols, k * channels : (k + 1) * channels] = mixed[
                k * cols : (k + 1) * cols
            ]


def matrices_kernel(block, cols, ahead_ref, back_ref, ahead_out, back_out):
    def body(row, carry):
        fill_matrices(ahead_ref, ahead_out, row, cols)
        fill_matrices(back_ref, back_out, row, cols)
        return carry

    lax.fori_loop(0, block, body, 0)


def add_outer(left, spread, grad_ref, step):
    part = lax.dot_general(
        left, spread, (((0,), (0,)), ((), ())), preferred_element_type=jnp.float32
    )

    @pl.when(step == 0)
    def _():
        grad_ref[...] = part

    @pl.when(step > 0)
    def _():
        grad_ref[...] += part


def first_kernel(block, own, low, high, matrix, weight, pre_out, act_out, spread_out):
    step = pl.program_id(0)
    spread_block(own, low, high, matrix, 0, spread_out, step * block, block)
    pre = jnp.dot(spread_out[...], weight[...], preferred_element_type=jnp.float32)
    pre_out[...] = pre
    act_out[...] = (pre * gelu_cdf(pre)).astype(jnp.bfloat16).reshape(act_out.shape)


def slope_kernel(
    block, scale, own, low, high, matrix, weight, pre, spread_one, gp_out, grad_out, spread, grad
):
    step = pl.program_id(0)
    spread_block(own, low, high, matrix, 0, spread, step * block, block)
    grad_act = jnp.dot(spread[...], weight[...], preferred_element_type=jnp.float32)
    gp = (grad_act * gelu_slope(pre[...])).astype(jnp.bfloat16)
    gp_out[...] = gp.reshape(gp_out.shape)
    add_outer(gp, spread_one[...], grad, step)

    @pl.when(step == pl.num_programs(0) - 1)
    def _():
        grad_out[...] = (grad[...] * scale).T.astype(jnp.bfloat16)


def second_kernel(
    block, scale, own, low, high, matrix, weight, resid, cot, mixed_out, grad_out, spread, grad
):
    step = pl.program_id(0)
    spread_block(own, low, high, matrix, 0, spread, step * block, block)
    branch = jnp.dot(spread[...], weight[...], preferred_element_type=jnp.float32)
    flat = branch.shape
    mixed_out[...] = (
        (resid[...].reshape(flat).astype(jnp.float32) + branch)
        .astype(jnp.bfloat16)
        .reshape(mixed_out.shape)
    )
    add_outer(cot[...].reshape(flat), spread[...], grad, step)

    @pl.when(step == pl.num_programs(0) - 1)
    def _():
        grad_out[...] = (grad[...] * scale).T.astype(jnp.bfloat16)


def last_kernel(block, own, low, high, matrix, weight, cot, field_out, spread):
    step = pl.program_id(0)
    spread_block(own, low, high, matrix, 0, spread, step * block, block)
    adj = jnp.dot(spread[...], weight[...], preferred_element_type=jnp.float32)
    field_out[...] = (
        (cot[...].reshape(adj.shape).astype(jnp.float32) + adj)
        .astype(jnp.bfloat16)
        .reshape(field_out.shape)
    )


def halos(field, halo):
    count = lax.axis_size("lon")
    cols = field.shape[1]
    forward = [(i, (i + 1) % count) for i in range(count)]
    backward = [(target, source) for source, target in forward]
    low = lax.ppermute(field[:, cols - halo :], "lon", forward)
    high = lax.ppermute(field[:, :halo], "lon", backward)
    return low, high


def on_device(
    activations, quadrature, support, support_count, weight_first, weight_second, cotangent
):
    rows, cols, channels = activations.shape
    kernels = weight_first.shape[0]
    halo = -(-(cols // 2) // 16) * 16
    block = 8
    steps = rows // block
    wide = kernels * channels
    scale = 1.0 / math.sqrt(rows * cols * lax.axis_size("lon"))
    flat_first = weight_first.reshape(wide, channels)
    flat_second = weight_second.reshape(wide, channels)
    turned_first = weight_first.swapaxes(1, 2).reshape(wide, channels)
    turned_second = weight_second.swapaxes(1, 2).reshape(wide, channels)
    ahead, back = tap_tables(quadrature, support, support_count, halo)

    params = pltpu.CompilerParams(vmem_limit_bytes=VMEM_LIMIT)
    bf16, f32 = jnp.bfloat16, jnp.float32
    whole = lambda shape: pl.BlockSpec(shape, lambda i: (0,) * len(shape))
    by_row = lambda shape: pl.BlockSpec(shape, lambda i: (i,) + (0,) * (len(shape) - 1))
    field_spec = by_row((block, cols, channels))
    matrix_spec = by_row((block, kernels * cols, 3 * LANES))
    common = [
        whole((rows, cols, channels)),
        whole((rows, halo, channels)),
        whole((rows, halo, channels)),
        matrix_spec,
        whole((wide, channels)),
    ]
    spread_shape = (block * cols, wide)
    field_type = jax.ShapeDtypeStruct((rows, cols, channels), bf16)
    grad_type = jax.ShapeDtypeStruct((wide, channels), bf16)
    work = [pltpu.VMEM(spread_shape, bf16), pltpu.VMEM((channels, wide), f32)]
    cost = pl.CostEstimate(flops=6 * 10**9, bytes_accessed=20 * 10**6, transcendentals=0)

    def call(body, **kw):
        return pl.pallas_call(
            body, grid=(steps,), compiler_params=params, cost_estimate=cost, **kw
        )

    matrix_type = jax.ShapeDtypeStruct((rows, kernels * cols, 3 * LANES), bf16)
    act_low, act_high = halos(activations, halo)
    cot_low, cot_high = halos(cotangent, halo)
    table_spec = by_row((block, kernels * 3, LANES))
    m_ahead, m_back = call(
        functools.partial(matrices_kernel, block, cols),
        in_specs=[table_spec, table_spec],
        out_specs=[matrix_spec, matrix_spec],
        out_shape=[matrix_type, matrix_type],
    )(ahead, back)
    cells = rows * cols
    pre, activated, spread_one = call(
        functools.partial(first_kernel, block),
        in_specs=common,
        out_specs=[by_row((block * cols, channels)), field_spec, by_row(spread_shape)],
        out_shape=[
            jax.ShapeDtypeStruct((cells, channels), f32),
            field_type,
            jax.ShapeDtypeStruct((cells, wide), bf16),
        ],
    )(activations, act_low, act_high, m_ahead, flat_first)
    mid_low, mid_high = halos(activated, halo)
    gp, grad_first = call(
        functools.partial(slope_kernel, block, scale),
        in_specs=common + [by_row((block * cols, channels)), by_row(spread_shape)],
        out_specs=[field_spec, whole((wide, channels))],
        out_shape=[field_type, grad_type],
        scratch_shapes=work,
    )(cotangent, cot_low, cot_high, m_back, turned_second, pre, spread_one)
    gp_low, gp_high = halos(gp, halo)
    total_first = lax.psum(grad_first, "lon")
    mixed, grad_second = call(
        functools.partial(second_kernel, block, scale),
        in_specs=common + [field_spec, field_spec],
        out_specs=[field_spec, whole((wide, channels))],
        out_shape=[field_type, grad_type],
        scratch_shapes=work,
    )(activated, mid_low, mid_high, m_ahead, flat_second, activations, cotangent)
    total_second = lax.psum(grad_second, "lon")
    grad_field = call(
        functools.partial(last_kernel, block),
        in_specs=common + [field_spec],
        out_specs=field_spec,
        out_shape=field_type,
        scratch_shapes=work[:1],
    )(gp, gp_low, gp_high, m_back, turned_first, cotangent)
    return (
        mixed,
        grad_field,
        total_first.astype(f32).reshape(kernels, channels, channels),
        total_second.astype(f32).reshape(kernels, channels, channels),
    )


def solution(mesh):
    placed = (P("ens", "lon", None), P(), P(), P(), P(), P(), P("ens", "lon", None))
    return jax.shard_map(
        on_device,
        mesh=mesh,
        in_specs=placed,
        out_specs=(
            P("ens", "lon", None),
            P("ens", "lon", None),
            P("ens", None, None),
            P("ens", None, None),
        ),
        check_vma=False,
    )
```

```python
import functools
import math

import jax
import jax.numpy as jnp
from jax import lax
from jax.experimental import pallas as pl
from jax.experimental.pallas import tpu as pltpu
from jax.sharding import PartitionSpec as P

LANES = 128
VMEM_LIMIT = 56 * 1024 * 1024


def gelu_cdf(value):
    return 0.5 + 0.5 * lax.erf(value * 0.7071067811865476)


def gelu_slope(value):
    density = jnp.exp(-0.5 * value * value) * 0.3989422804014327
    return gelu_cdf(value) + value * density


def tap_tables(quadrature, support, support_count, halo):
    kernel_count, rows, taps, slots = quadrature.shape
    bands = support.shape[0]
    band_rows = rows // bands
    live = lax.broadcasted_iota(jnp.int32, support.shape, 1) < support_count[:, None]
    lane = jnp.arange(LANES, dtype=jnp.int32)
    by_band = quadrature.reshape(kernel_count, bands, band_rows, taps, slots)

    def place(sign):
        hot = ((halo + sign * support)[:, :, None] == lane) & live[:, :, None]
        table = jnp.einsum(
            "kbrds,bsl->brkdl", by_band, hot.astype(jnp.bfloat16), preferred_element_type=jnp.float32
        )
        return table.reshape(rows, kernel_count, taps, LANES)

    row = jnp.arange(rows)[:, None, None, None]
    tap = jnp.arange(taps)[None, None, :, None]
    inside = (row + tap >= 1) & (row + tap <= rows)
    ahead = jnp.where(inside, place(1), 0.0)
    source = jnp.pad(place(-1), ((1, 1), (0, 0), (0, 0), (0, 0)))
    back = jnp.stack([source[e : e + rows, :, taps - 1 - e] for e in range(taps)], 2)
    shape = (rows, kernel_count * taps, LANES)
    return ahead.reshape(shape), back.reshape(shape)


def fill_matrices(table_ref, matrix_ref, row, cols):
    table = table_ref[row]
    for k in range(table.shape[0] // 3):
        for d in range(3):
            line = jnp.broadcast_to(table[k * 3 + d][None], (cols, LANES))
            rolled = pltpu.roll(line, 0, 1, stride=1, stride_axis=0)
            matrix_ref[row, k * cols : (k + 1) * cols, d * LANES : (d + 1) * LANES] = rolled.astype(
                jnp.bfloat16
            )


def spread_block(own, low, high, matrix, matrix_row, spread, first_row, count):
    rows, cols, channels = own.shape
    filler = jnp.zeros((LANES - cols - 2 * low.shape[1], channels), jnp.bfloat16)
    for r in range(count):
        parts = []
        for d in range(3):
            src = jnp.clip(first_row + r + d - 1, 0, rows - 1)
            parts += [low[src], own[src], high[src], filler]
        mixed = jnp.dot(
            matrix[matrix_row + r],
            jnp.concatenate(parts, 0),
            preferred_element_type=jnp.float32,
        ).astype(jnp.bfloat16)
        for k in range(mixed.shape[0] // cols):
            spread[r * cols : (r + 1) * cols, k * channels : (k + 1) * channels] = mixed[
                k * cols : (k + 1) * cols
            ]


def greet(partners):
    barrier = pltpu.get_barrier_semaphore()
    for other in partners:
        pl.semaphore_signal(
            barrier, inc=1, device_id={"lon": other}, device_id_type=pl.DeviceIdType.MESH
        )
    pl.semaphore_wait(barrier, len(partners))


def send(src, dst, send_sem, recv_sem, other):
    return pltpu.make_async_remote_copy(
        src_ref=src,
        dst_ref=dst,
        send_sem=send_sem,
        recv_sem=recv_sem,
        device_id={"lon": other},
        device_id_type=pl.DeviceIdType.MESH,
    )


def sides(size):
    me = lax.axis_index("lon")
    return [lax.rem(me + 1, size), lax.rem(me + size - 1, size)]


def edge_copies(size, field, low, high, sems):
    right, left = sides(size)
    cols, halo = field.shape[1], low.shape[1]
    return [
        send(field.at[:, pl.ds(cols - halo, halo)], low, sems.at[0], sems.at[1], right),
        send(field.at[:, pl.ds(0, halo)], high, sems.at[2], sems.at[3], left),
    ]


def with_edges(size, body, spots, *refs):
    *refs, sems = refs
    field, low, high = (refs[spot] for spot in spots)
    step = pl.program_id(0)

    @pl.when(step == 0)
    def _():
        greet(sides(size))
        for copy in edge_copies(size, field, low, high, sems):
            copy.start()

    body(*[ref for spot, ref in enumerate(refs) if spot not in spots])

    @pl.when(step == pl.num_programs(0) - 1)
    def _():
        for copy in edge_copies(size, field, low, high, sems):
            copy.wait()


def partners_of(size):
    me = lax.axis_index("lon")
    bit0, bit1 = lax.rem(me, 2), lax.rem(me // 2, 2)
    return [me + 1 - 2 * bit0, me + 2 - 4 * bit1] + [
        lax.rem(me + 4 * t, size) for t in range(1, size // 4)
    ]


def sum_stages(size, local, buffers, total, sems):
    got_half, half, got_quarter, quarter, got_piece, full = buffers
    me = lax.axis_index("lon")
    bit0, bit1, rank = lax.rem(me, 2), lax.rem(me // 2, 2), me // 4
    group = size // 4
    rows = local.shape[0]
    r2, r4, rp = rows // 2, rows // 4, rows // size
    others = partners_of(size)
    part = lambda ref, start, count: ref.at[pl.ds(pl.multiple_of(start, 16), count)]
    f32 = jnp.float32
    base0 = bit0 * r2
    base1 = base0 + bit1 * r4
    base2 = base1 + rank * rp
    pair = lambda i: (sems.at[2 * i], sems.at[2 * i + 1])

    halves = [send(part(local, (1 - bit0) * r2, r2), got_half, *pair(0), others[0])]
    quarters = [send(part(half, (1 - bit1) * r4, r4), got_quarter, *pair(1), others[1])]
    pieces, spreads = [], []
    for t in range(1, group):
        target = lax.rem(rank + t, group)
        pieces.append(
            send(part(quarter, target * rp, rp), got_piece.at[t - 1], *pair(3 + t), others[1 + t])
        )
        mine = part(full, base2, rp)
        spreads.append(send(mine, mine, *pair(2 + group + t), others[1 + t]))
    mine1, mine0 = part(full, base1, r4), part(full, base0, r2)
    back1 = [send(mine1, mine1, *pair(2), others[1])]
    back0 = [send(mine0, mine0, *pair(3), others[0])]

    def add_half():
        half[...] = (part(local, base0, r2)[...].astype(f32) + got_half[...].astype(f32)).astype(
            jnp.bfloat16
        )

    def add_quarter():
        quarter[...] = (
            part(half, bit1 * r4, r4)[...].astype(f32) + got_quarter[...].astype(f32)
        ).astype(jnp.bfloat16)

    def add_pieces():
        acc = part(quarter, rank * rp, rp)[...].astype(f32)
        for t in range(group - 1):
            acc = acc + got_piece[t].astype(f32)
        full[pl.ds(pl.multiple_of(base2, 16), rp), :] = acc.astype(jnp.bfloat16)

    def finish():
        total[...] = full[...].astype(f32)

    waits = [[], halves, quarters, pieces, spreads, back1, back0]
    works = [None, add_half, add_quarter, add_pieces, None, None, finish]
    starts = [halves, quarters, pieces, spreads, back1, back0, []]

    def stage(number):
        def run():
            for copy in waits[number]:
                copy.wait()
            if works[number] is not None:
                works[number]()
            for copy in starts[number]:
                copy.start()

        return run

    return [stage(number) for number in range(7)]


def sum_scratch(rows, channels, size):
    dims = [(rows // 2,), (rows // 2,), (rows // 4,), (rows // 4,), (size // 4 - 1, rows // size), (rows,)]
    return [pltpu.VMEM(dim + (channels,), jnp.bfloat16) for dim in dims] + [
        pltpu.SemaphoreType.DMA((2 * (2 + 2 * (size // 4)),))
    ]


SUM_STEPS = (0, 1, 2, 4, 6, 7)


def run_stages(stages, step):
    for number, when in enumerate(SUM_STEPS):
        pl.when(step == when)(stages[number])


def matrices_kernel(block, cols, ahead_ref, back_ref, ahead_out, back_out):
    def body(row, carry):
        fill_matrices(ahead_ref, ahead_out, row, cols)
        fill_matrices(back_ref, back_out, row, cols)
        return carry

    lax.fori_loop(0, block, body, 0)


def add_outer(left, spread, grad_ref, step):
    part = lax.dot_general(
        left, spread, (((0,), (0,)), ((), ())), preferred_element_type=jnp.float32
    )

    @pl.when(step == 0)
    def _():
        grad_ref[...] = part

    @pl.when(step > 0)
    def _():
        grad_ref[...] += part


def first_kernel(block, own, low, high, matrix, weight, pre_out, act_out, spread_out):
    step = pl.program_id(0)
    spread_block(own, low, high, matrix, 0, spread_out, step * block, block)
    pre = jnp.dot(spread_out[...], weight[...], preferred_element_type=jnp.float32)
    pre_out[...] = pre
    act_out[...] = (pre * gelu_cdf(pre)).astype(jnp.bfloat16).reshape(act_out.shape)


def slope_kernel(
    block, scale, own, low, high, matrix, weight, pre, spread_one, gp_out, grad_out, spread, grad
):
    step = pl.program_id(0)
    spread_block(own, low, high, matrix, 0, spread, step * block, block)
    grad_act = jnp.dot(spread[...], weight[...], preferred_element_type=jnp.float32)
    gp = (grad_act * gelu_slope(pre[...])).astype(jnp.bfloat16)
    gp_out[...] = gp.reshape(gp_out.shape)
    add_outer(gp, spread_one[...], grad, step)

    @pl.when(step == pl.num_programs(0) - 1)
    def _():
        grad_out[...] = (grad[...] * scale).T.astype(jnp.bfloat16)


def second_kernel(
    size, block, scale, own, low, high, matrix, weight, resid, cot, local, edge_field,
    mixed_out, grad_out, total_out, edge_low, edge_high, spread, grad, *work
):
    step = pl.program_id(0)
    *buffers, sum_sems, edge_sems = work
    stages = sum_stages(size, local, buffers, total_out, sum_sems)

    @pl.when(step == 0)
    def _():
        greet(sides(size) + partners_of(size))
        for copy in edge_copies(size, edge_field, edge_low, edge_high, edge_sems):
            copy.start()

    run_stages(stages, step)
    spread_block(own, low, high, matrix, 0, spread, step * block, block)
    branch = jnp.dot(spread[...], weight[...], preferred_element_type=jnp.float32)
    flat = branch.shape
    mixed_out[...] = (
        (resid[...].reshape(flat).astype(jnp.float32) + branch)
        .astype(jnp.bfloat16)
        .reshape(mixed_out.shape)
    )
    add_outer(cot[...].reshape(flat), spread[...], grad, step)

    @pl.when(step == pl.num_programs(0) - 1)
    def _():
        grad_out[...] = (grad[...] * scale).T.astype(jnp.bfloat16)
        stages[-1]()
        for copy in edge_copies(size, edge_field, edge_low, edge_high, edge_sems):
            copy.wait()


def last_kernel(
    size, block, own, low, high, matrix, weight, cot, local, field_out, total_out, spread, *work
):
    step = pl.program_id(0)
    *buffers, sum_sems = work
    stages = sum_stages(size, local, buffers, total_out, sum_sems)

    @pl.when(step == 0)
    def _():
        greet(partners_of(size))

    run_stages(stages, step)
    spread_block(own, low, high, matrix, 0, spread, step * block, block)
    adj = jnp.dot(spread[...], weight[...], preferred_element_type=jnp.float32)
    field_out[...] = (
        (cot[...].reshape(adj.shape).astype(jnp.float32) + adj)
        .astype(jnp.bfloat16)
        .reshape(field_out.shape)
    )

    @pl.when(step == pl.num_programs(0) - 1)
    def _():
        stages[-1]()


def on_device(
    activations, quadrature, support, support_count, weight_first, weight_second, cotangent
):
    rows, cols, channels = activations.shape
    kernels = weight_first.shape[0]
    halo = -(-(cols // 2) // 16) * 16
    block = 8
    steps = rows // block
    wide = kernels * channels
    scale = 1.0 / math.sqrt(rows * cols * lax.axis_size("lon"))
    flat_first = weight_first.reshape(wide, channels)
    flat_second = weight_second.reshape(wide, channels)
    turned_first = weight_first.swapaxes(1, 2).reshape(wide, channels)
    turned_second = weight_second.swapaxes(1, 2).reshape(wide, channels)
    ahead, back = tap_tables(quadrature, support, support_count, halo)

    bf16, f32 = jnp.bfloat16, jnp.float32
    whole = lambda shape: pl.BlockSpec(shape, lambda i: (0,) * len(shape))
    by_row = lambda shape: pl.BlockSpec(shape, lambda i: (i,) + (0,) * (len(shape) - 1))
    field_spec = by_row((block, cols, channels))
    matrix_spec = by_row((block, kernels * cols, 3 * LANES))
    common = [
        whole((rows, cols, channels)),
        whole((rows, halo, channels)),
        whole((rows, halo, channels)),
        matrix_spec,
        whole((wide, channels)),
    ]
    spread_shape = (block * cols, wide)
    field_type = jax.ShapeDtypeStruct((rows, cols, channels), bf16)
    grad_type = jax.ShapeDtypeStruct((wide, channels), bf16)
    work = [pltpu.VMEM(spread_shape, bf16), pltpu.VMEM((channels, wide), f32)]
    size = lax.axis_size("lon")
    assert steps == 8 and size % 4 == 0

    def call(number, body, **kw):
        return pl.pallas_call(
            body,
            grid=(steps,),
            compiler_params=pltpu.CompilerParams(
                vmem_limit_bytes=VMEM_LIMIT, collective_id=number, has_side_effects=True
            ),
            **kw,
        )

    matrix_type = jax.ShapeDtypeStruct((rows, kernels * cols, 3 * LANES), bf16)
    halo_type = jax.ShapeDtypeStruct((rows, halo, channels), bf16)
    total_type = jax.ShapeDtypeStruct((wide, channels), f32)
    anywhere = pl.BlockSpec(memory_space=pl.ANY)
    edge_sems = pltpu.SemaphoreType.DMA((4,))
    table_spec = by_row((block, kernels * 3, LANES))
    m_ahead, m_back, act_low, act_high = call(
        0,
        functools.partial(
            with_edges, size, functools.partial(matrices_kernel, block, cols), (2, 5, 6)
        ),
        in_specs=[table_spec, table_spec, anywhere],
        out_specs=[matrix_spec, matrix_spec, anywhere, anywhere],
        out_shape=[matrix_type, matrix_type, halo_type, halo_type],
        scratch_shapes=[edge_sems],
    )(ahead, back, activations)
    cells = rows * cols
    pre, activated, spread_one, cot_low, cot_high = call(
        1,
        functools.partial(with_edges, size, functools.partial(first_kernel, block), (5, 9, 10)),
        in_specs=common + [anywhere],
        out_specs=[
            by_row((block * cols, channels)), field_spec, by_row(spread_shape), anywhere, anywhere
        ],
        out_shape=[
            jax.ShapeDtypeStruct((cells, channels), f32),
            field_type,
            jax.ShapeDtypeStruct((cells, wide), bf16),
            halo_type,
            halo_type,
        ],
        scratch_shapes=[edge_sems],
    )(activations, act_low, act_high, m_ahead, flat_first, cotangent)
    gp, grad_first, mid_low, mid_high = call(
        2,
        functools.partial(
            with_edges, size, functools.partial(slope_kernel, block, scale), (7, 10, 11)
        ),
        in_specs=common + [by_row((block * cols, channels)), by_row(spread_shape), anywhere],
        out_specs=[field_spec, whole((wide, channels)), anywhere, anywhere],
        out_shape=[field_type, grad_type, halo_type, halo_type],
        scratch_shapes=work + [edge_sems],
    )(cotangent, cot_low, cot_high, m_back, turned_second, pre, spread_one, activated)
    mixed, grad_second, total_first, gp_low, gp_high = call(
        3,
        functools.partial(second_kernel, size, block, scale),
        in_specs=common + [field_spec, field_spec, whole((wide, channels)), anywhere],
        out_specs=[
            field_spec, whole((wide, channels)), whole((wide, channels)), anywhere, anywhere
        ],
        out_shape=[field_type, grad_type, total_type, halo_type, halo_type],
        scratch_shapes=work + sum_scratch(wide, channels, size) + [edge_sems],
    )(activated, mid_low, mid_high, m_ahead, flat_second, activations, cotangent, grad_first, gp)
    grad_field, total_second = call(
        4,
        functools.partial(last_kernel, size, block),
        in_specs=common + [field_spec, whole((wide, channels))],
        out_specs=[field_spec, whole((wide, channels))],
        out_shape=[field_type, total_type],
        scratch_shapes=work[:1] + sum_scratch(wide, channels, size),
    )(gp, gp_low, gp_high, m_back, turned_first, cotangent, grad_second)
    return (
        mixed,
        grad_field,
        total_first.reshape(kernels, channels, channels),
        total_second.reshape(kernels, channels, channels),
    )


def solution(mesh):
    placed = (P("ens", "lon", None), P(), P(), P(), P(), P(), P("ens", "lon", None))
    return jax.shard_map(
        on_device,
        mesh=mesh,
        in_specs=placed,
        out_specs=(
            P("ens", "lon", None),
            P("ens", "lon", None),
            P("ens", None, None),
            P("ens", None, None),
        ),
        check_vma=False,
    )
```

```python
import functools
import math

import jax
import jax.numpy as jnp
from jax import lax
from jax.experimental import pallas as pl
from jax.experimental.pallas import tpu as pltpu
from jax.sharding import PartitionSpec as P

LANES = 128
VMEM_LIMIT = 56 * 1024 * 1024


def gelu_cdf(value):
    return 0.5 + 0.5 * lax.erf(value * 0.7071067811865476)


def gelu_slope(value):
    density = jnp.exp(-0.5 * value * value) * 0.3989422804014327
    return gelu_cdf(value) + value * density


def tap_tables(quadrature, support, support_count, halo):
    kernel_count, rows, taps, slots = quadrature.shape
    bands = support.shape[0]
    band_rows = rows // bands
    live = lax.broadcasted_iota(jnp.int32, support.shape, 1) < support_count[:, None]
    lane = jnp.arange(LANES, dtype=jnp.int32)
    by_band = quadrature.reshape(kernel_count, bands, band_rows, taps, slots)

    def place(sign):
        hot = ((halo + sign * support)[:, :, None] == lane) & live[:, :, None]
        table = jnp.einsum(
            "kbrds,bsl->brkdl", by_band, hot.astype(jnp.bfloat16), preferred_element_type=jnp.float32
        )
        return table.reshape(rows, kernel_count, taps, LANES)

    row = jnp.arange(rows)[:, None, None, None]
    tap = jnp.arange(taps)[None, None, :, None]
    inside = (row + tap >= 1) & (row + tap <= rows)
    ahead = jnp.where(inside, place(1), 0.0)
    source = jnp.pad(place(-1), ((1, 1), (0, 0), (0, 0), (0, 0)))
    back = jnp.stack([source[e : e + rows, :, taps - 1 - e] for e in range(taps)], 2)
    shape = (rows, kernel_count * taps, LANES)
    return ahead.reshape(shape), back.reshape(shape)


def fill_matrices(table_ref, matrix_ref, row, cols):
    table = table_ref[row]
    for k in range(table.shape[0] // 3):
        for d in range(3):
            line = jnp.broadcast_to(table[k * 3 + d][None], (cols, LANES))
            rolled = pltpu.roll(line, 0, 1, stride=1, stride_axis=0)
            matrix_ref[row, k * cols : (k + 1) * cols, d * LANES : (d + 1) * LANES] = rolled.astype(
                jnp.bfloat16
            )


def spread_block(own, low, high, matrix, matrix_row, spread, first_row, count):
    rows, cols, channels = own.shape
    filler = jnp.zeros((LANES - cols - 2 * low.shape[1], channels), jnp.bfloat16)
    for r in range(count):
        parts = []
        for d in range(3):
            src = jnp.clip(first_row + r + d - 1, 0, rows - 1)
            parts += [low[src], own[src], high[src], filler]
        mixed = jnp.dot(
            matrix[matrix_row + r],
            jnp.concatenate(parts, 0),
            preferred_element_type=jnp.float32,
        ).astype(jnp.bfloat16)
        for k in range(mixed.shape[0] // cols):
            spread[r * cols : (r + 1) * cols, k * channels : (k + 1) * channels] = mixed[
                k * cols : (k + 1) * cols
            ]


def greet(partners):
    barrier = pltpu.get_barrier_semaphore()
    for other in partners:
        pl.semaphore_signal(
            barrier, inc=1, device_id={"lon": other}, device_id_type=pl.DeviceIdType.MESH
        )
    pl.semaphore_wait(barrier, len(partners))


def send(src, dst, send_sem, recv_sem, other):
    return pltpu.make_async_remote_copy(
        src_ref=src,
        dst_ref=dst,
        send_sem=send_sem,
        recv_sem=recv_sem,
        device_id={"lon": other},
        device_id_type=pl.DeviceIdType.MESH,
    )


def sides(size):
    me = lax.axis_index("lon")
    return [lax.rem(me + 1, size), lax.rem(me + size - 1, size)]


NARROW = 16


def pack_edges(field, to_right, to_left):
    cols = field.shape[1]
    pairs, width = to_right.shape[0], to_right.shape[1] // 2
    first = field.shape[0] - 2 * pairs
    for p in range(pairs):
        two = [field[first + 2 * p], field[first + 2 * p + 1]]
        to_right[p] = jnp.concatenate([row[cols - width :] for row in two], 0)
        to_left[p] = jnp.concatenate([row[:width] for row in two], 0)


def unpack_edges(edges, low, high):
    near_low, near_high, far_low, far_high = edges
    near, halo, channels = near_low.shape[0], low.shape[1], low.shape[2]
    pairs, width = far_low.shape[0], far_low.shape[1] // 2
    blank = jnp.zeros((near, halo - NARROW, channels), low.dtype)
    low[:near, : halo - NARROW] = blank
    low[:near, halo - NARROW :] = near_low[...]
    high[:near, :NARROW] = near_high[...]
    high[:near, NARROW:] = blank
    blank = jnp.zeros((halo - width, channels), low.dtype)
    for p in range(pairs):
        below, above = far_low[p], far_high[p]
        for q in range(2):
            cut = slice(q * width, (q + 1) * width)
            low[near + 2 * p + q] = jnp.concatenate([blank, below[cut]], 0)
            high[near + 2 * p + q] = jnp.concatenate([above[cut], blank], 0)


def edge_copies(size, field, to_right, to_left, edges, sems):
    right, left = sides(size)
    near_low, near_high, far_low, far_high = edges
    cols, near = field.shape[1], near_low.shape[0]
    rows = pl.ds(0, near)
    return [
        send(field.at[rows, pl.ds(cols - NARROW, NARROW)], near_low, sems.at[0], sems.at[1], right),
        send(field.at[rows, pl.ds(0, NARROW)], near_high, sems.at[2], sems.at[3], left),
        send(to_right, far_low, sems.at[4], sems.at[5], right),
        send(to_left, far_high, sems.at[6], sems.at[7], left),
    ]


def with_edges(size, body, at_field, at_edges, *refs):
    *refs, to_right, to_left, sems = refs
    field, edges = refs[at_field], refs[at_edges : at_edges + 4]
    step = pl.program_id(0)

    @pl.when(step == 0)
    def _():
        pack_edges(field, to_right, to_left)
        greet(sides(size))
        for copy in edge_copies(size, field, to_right, to_left, edges, sems):
            copy.start()

    body(*refs[:at_field], *refs[at_field + 1 : at_edges], *refs[at_edges + 4 :])

    @pl.when(step == pl.num_programs(0) - 1)
    def _():
        for copy in edge_copies(size, field, to_right, to_left, edges, sems):
            copy.wait()


def partners_of(size):
    me = lax.axis_index("lon")
    bit0, bit1 = lax.rem(me, 2), lax.rem(me // 2, 2)
    return [me + 1 - 2 * bit0, me + 2 - 4 * bit1] + [
        lax.rem(me + 4 * t, size) for t in range(1, size // 4)
    ]


def sum_stages(size, local, buffers, total, sems):
    got_half, half, got_quarter, quarter, got_piece, full = buffers
    me = lax.axis_index("lon")
    bit0, bit1, rank = lax.rem(me, 2), lax.rem(me // 2, 2), me // 4
    group = size // 4
    rows = local.shape[0]
    r2, r4, rp = rows // 2, rows // 4, rows // size
    others = partners_of(size)
    part = lambda ref, start, count: ref.at[pl.ds(pl.multiple_of(start, 16), count)]
    f32 = jnp.float32
    base0 = bit0 * r2
    base1 = base0 + bit1 * r4
    base2 = base1 + rank * rp
    pair = lambda i: (sems.at[2 * i], sems.at[2 * i + 1])

    halves = [send(part(local, (1 - bit0) * r2, r2), got_half, *pair(0), others[0])]
    quarters = [send(part(half, (1 - bit1) * r4, r4), got_quarter, *pair(1), others[1])]
    pieces, spreads = [], []
    for t in range(1, group):
        target = lax.rem(rank + t, group)
        pieces.append(
            send(part(quarter, target * rp, rp), got_piece.at[t - 1], *pair(3 + t), others[1 + t])
        )
        mine = part(full, base2, rp)
        spreads.append(send(mine, mine, *pair(2 + group + t), others[1 + t]))
    mine1, mine0 = part(full, base1, r4), part(full, base0, r2)
    back1 = [send(mine1, mine1, *pair(2), others[1])]
    back0 = [send(mine0, mine0, *pair(3), others[0])]

    def add_half():
        half[...] = (part(local, base0, r2)[...].astype(f32) + got_half[...].astype(f32)).astype(
            jnp.bfloat16
        )

    def add_quarter():
        quarter[...] = (
            part(half, bit1 * r4, r4)[...].astype(f32) + got_quarter[...].astype(f32)
        ).astype(jnp.bfloat16)

    def add_pieces():
        acc = part(quarter, rank * rp, rp)[...].astype(f32)
        for t in range(group - 1):
            acc = acc + got_piece[t].astype(f32)
        full[pl.ds(pl.multiple_of(base2, 16), rp), :] = acc.astype(jnp.bfloat16)

    def finish():
        total[0][...] = full[: rows // 2].astype(f32)
        total[1][...] = full[rows // 2 :].astype(f32)

    waits = [[], halves, quarters, pieces, spreads, back1, back0]
    works = [None, add_half, add_quarter, add_pieces, None, None, finish]
    starts = [halves, quarters, pieces, spreads, back1, back0, []]

    def stage(number):
        def run():
            for copy in waits[number]:
                copy.wait()
            if works[number] is not None:
                works[number]()
            for copy in starts[number]:
                copy.start()

        return run

    return [stage(number) for number in range(7)]


def sum_scratch(rows, channels, size):
    dims = [(rows // 2,), (rows // 2,), (rows // 4,), (rows // 4,), (size // 4 - 1, rows // size), (rows,)]
    return [pltpu.VMEM(dim + (channels,), jnp.bfloat16) for dim in dims] + [
        pltpu.SemaphoreType.DMA((2 * (2 + 2 * (size // 4)),))
    ]


SUM_STEPS = (1, 3, 5, 6, 7)


def run_stages(stages, step):
    for number, when in enumerate(SUM_STEPS, 1):
        pl.when(step == when)(stages[number])


def matrices_kernel(block, cols, ahead_ref, back_ref, ahead_out, back_out):
    def body(row, carry):
        fill_matrices(ahead_ref, ahead_out, row, cols)
        fill_matrices(back_ref, back_out, row, cols)
        return carry

    lax.fori_loop(0, block, body, 0)


def add_outer(left, spread, grad_ref, step):
    part = lax.dot_general(
        left, spread, (((0,), (0,)), ((), ())), preferred_element_type=jnp.float32
    )

    @pl.when(step == 0)
    def _():
        grad_ref[...] = part

    @pl.when(step > 0)
    def _():
        grad_ref[...] += part


def first_kernel(block, own, e0, e1, e2, e3, matrix, weight, pre_out, act_out, spread_out, low, high):
    step = pl.program_id(0)
    pl.when(step == 0)(lambda: unpack_edges((e0, e1, e2, e3), low, high))
    spread_block(own, low, high, matrix, 0, spread_out, step * block, block)
    pre = jnp.dot(spread_out[...], weight[...], preferred_element_type=jnp.float32)
    pre_out[...] = pre
    act_out[...] = (pre * gelu_cdf(pre)).astype(jnp.bfloat16).reshape(act_out.shape)


def slope_kernel(
    block, scale, own, e0, e1, e2, e3, matrix, weight, pre, spread_one, gp_out, grad_out,
    low, high, spread, grad,
):
    step = pl.program_id(0)
    pl.when(step == 0)(lambda: unpack_edges((e0, e1, e2, e3), low, high))
    spread_block(own, low, high, matrix, 0, spread, step * block, block)
    grad_act = jnp.dot(spread[...], weight[...], preferred_element_type=jnp.float32)
    gp = (grad_act * gelu_slope(pre[...])).astype(jnp.bfloat16)
    gp_out[...] = gp.reshape(gp_out.shape)
    add_outer(gp, spread_one[...], grad, step)

    @pl.when(step == pl.num_programs(0) - 1)
    def _():
        grad_out[...] = (grad[...] * scale).T.astype(jnp.bfloat16)


def second_kernel(
    block, scale, own, e0, e1, e2, e3, matrix, weight, resid, cot, mixed_out, grad_out,
    low, high, spread, grad,
):
    step = pl.program_id(0)
    pl.when(step == 0)(lambda: unpack_edges((e0, e1, e2, e3), low, high))
    spread_block(own, low, high, matrix, 0, spread, step * block, block)
    branch = jnp.dot(spread[...], weight[...], preferred_element_type=jnp.float32)
    flat = branch.shape
    mixed_out[...] = (
        (resid[...].reshape(flat).astype(jnp.float32) + branch)
        .astype(jnp.bfloat16)
        .reshape(mixed_out.shape)
    )
    add_outer(cot[...].reshape(flat), spread[...], grad, step)

    @pl.when(step == pl.num_programs(0) - 1)
    def _():
        grad_out[...] = (grad[...] * scale).T.astype(jnp.bfloat16)


def last_kernel(
    size, block, own, e0, e1, e2, e3, matrix, weight, cot, grad_first, grad_second,
    field_out, total_first, total_second, low, high, spread, local, *work
):
    step = pl.program_id(0)
    *buffers, sum_sems = work
    wide = grad_first.shape[0]
    stages = sum_stages(size, local, buffers, (total_first, total_second), sum_sems)

    @pl.when(step == 0)
    def _():
        local[:wide] = grad_first[...]
        local[wide:] = grad_second[...]
        greet(partners_of(size))
        stages[0]()
        unpack_edges((e0, e1, e2, e3), low, high)

    run_stages(stages, step)
    spread_block(own, low, high, matrix, 0, spread, step * block, block)
    adj = jnp.dot(spread[...], weight[...], preferred_element_type=jnp.float32)
    field_out[...] = (
        (cot[...].reshape(adj.shape).astype(jnp.float32) + adj)
        .astype(jnp.bfloat16)
        .reshape(field_out.shape)
    )

    @pl.when(step == pl.num_programs(0) - 1)
    def _():
        stages[-1]()


def on_device(
    activations, quadrature, support, support_count, weight_first, weight_second, cotangent
):
    rows, cols, channels = activations.shape
    kernels = weight_first.shape[0]
    halo = -(-(cols // 2) // 16) * 16
    block = 8
    steps = rows // block
    wide = kernels * channels
    scale = 1.0 / math.sqrt(rows * cols * lax.axis_size("lon"))
    flat_first = weight_first.reshape(wide, channels)
    flat_second = weight_second.reshape(wide, channels)
    turned_first = weight_first.swapaxes(1, 2).reshape(wide, channels)
    turned_second = weight_second.swapaxes(1, 2).reshape(wide, channels)
    ahead, back = tap_tables(quadrature, support, support_count, halo)

    bf16, f32 = jnp.bfloat16, jnp.float32
    whole = lambda shape: pl.BlockSpec(shape, lambda i: (0,) * len(shape))
    by_row = lambda shape: pl.BlockSpec(shape, lambda i: (i,) + (0,) * (len(shape) - 1))
    field_spec = by_row((block, cols, channels))
    matrix_spec = by_row((block, kernels * cols, 3 * LANES))
    bands = support.shape[0]
    wider = [b for b in range(bands) if (cols // 2) * (b + 1) // bands > NARROW]
    near = max((min(wider) * (rows // bands) - 1) // 2 * 2, 2)
    near_shape = (near, NARROW, channels)
    far_shape = ((rows - near) // 2, 2 * (cols // 2), channels)
    edge_shapes = [near_shape, near_shape, far_shape, far_shape]
    common = (
        [whole((rows, cols, channels))]
        + [whole(shape) for shape in edge_shapes]
        + [matrix_spec, whole((wide, channels))]
    )
    spread_shape = (block * cols, wide)
    field_type = jax.ShapeDtypeStruct((rows, cols, channels), bf16)
    grad_type = jax.ShapeDtypeStruct((wide, channels), bf16)
    work = [pltpu.VMEM(spread_shape, bf16), pltpu.VMEM((channels, wide), f32)]
    size = lax.axis_size("lon")
    assert steps == 8 and size % 4 == 0

    def call(number, body, **kw):
        return pl.pallas_call(
            body,
            grid=(steps,),
            compiler_params=pltpu.CompilerParams(
                vmem_limit_bytes=VMEM_LIMIT, collective_id=number, has_side_effects=True
            ),
            **kw,
        )

    matrix_type = jax.ShapeDtypeStruct((rows, kernels * cols, 3 * LANES), bf16)
    edge_types = [jax.ShapeDtypeStruct(shape, bf16) for shape in edge_shapes]
    field_whole = whole((rows, cols, channels))
    unpacked = [pltpu.VMEM((rows, halo, channels), bf16)] * 2
    total_type = jax.ShapeDtypeStruct((wide, channels), f32)
    anywhere = pl.BlockSpec(memory_space=pl.ANY)
    edge_work = [pltpu.VMEM(far_shape, bf16)] * 2 + [pltpu.SemaphoreType.DMA((8,))]
    table_spec = by_row((block, kernels * 3, LANES))
    edged = lambda body, at_field, at_edges: functools.partial(
        with_edges, size, body, at_field, at_edges
    )
    m_ahead, m_back, *act_edges = call(
        0,
        edged(functools.partial(matrices_kernel, block, cols), 2, 5),
        in_specs=[table_spec, table_spec, field_whole],
        out_specs=[matrix_spec, matrix_spec] + [anywhere] * 4,
        out_shape=[matrix_type, matrix_type] + edge_types,
        scratch_shapes=edge_work,
    )(ahead, back, activations)
    cells = rows * cols
    pre, activated, spread_one, *cot_edges = call(
        1,
        edged(functools.partial(first_kernel, block), 7, 11),
        in_specs=common + [field_whole],
        out_specs=[by_row((block * cols, channels)), field_spec, by_row(spread_shape)]
        + [anywhere] * 4,
        out_shape=[
            jax.ShapeDtypeStruct((cells, channels), f32),
            field_type,
            jax.ShapeDtypeStruct((cells, wide), bf16),
        ]
        + edge_types,
        scratch_shapes=unpacked + edge_work,
    )(activations, *act_edges, m_ahead, flat_first, cotangent)
    gp, grad_first, *mid_edges = call(
        2,
        edged(functools.partial(slope_kernel, block, scale), 9, 12),
        in_specs=common + [by_row((block * cols, channels)), by_row(spread_shape), field_whole],
        out_specs=[field_spec, whole((wide, channels))] + [anywhere] * 4,
        out_shape=[field_type, grad_type] + edge_types,
        scratch_shapes=unpacked + work + edge_work,
    )(cotangent, *cot_edges, m_back, turned_second, pre, spread_one, activated)
    mixed, grad_second, *gp_edges = call(
        3,
        edged(functools.partial(second_kernel, block, scale), 9, 12),
        in_specs=common + [field_spec, field_spec, field_whole],
        out_specs=[field_spec, whole((wide, channels))] + [anywhere] * 4,
        out_shape=[field_type, grad_type] + edge_types,
        scratch_shapes=unpacked + work + edge_work,
    )(activated, *mid_edges, m_ahead, flat_second, activations, cotangent, gp)
    grad_spec = whole((wide, channels))
    grad_field, total_first, total_second = call(
        4,
        functools.partial(last_kernel, size, block),
        in_specs=common + [field_spec, grad_spec, grad_spec],
        out_specs=[field_spec, grad_spec, grad_spec],
        out_shape=[field_type, total_type, total_type],
        scratch_shapes=unpacked
        + work[:1]
        + [pltpu.VMEM((2 * wide, channels), bf16)]
        + sum_scratch(2 * wide, channels, size),
    )(gp, *gp_edges, m_back, turned_first, cotangent, grad_first, grad_second)
    return (
        mixed,
        grad_field,
        total_first.reshape(kernels, channels, channels),
        total_second.reshape(kernels, channels, channels),
    )


def solution(mesh):
    placed = (P("ens", "lon", None), P(), P(), P(), P(), P(), P("ens", "lon", None))
    return jax.shard_map(
        on_device,
        mesh=mesh,
        in_specs=placed,
        out_specs=(
            P("ens", "lon", None),
            P("ens", "lon", None),
            P("ens", None, None),
            P("ens", None, None),
        ),
        check_vma=False,
    )
```

```python
import functools
import math

import jax
import jax.numpy as jnp
from jax import lax
from jax.experimental import pallas as pl
from jax.experimental.pallas import tpu as pltpu
from jax.sharding import PartitionSpec as P

LANES = 128
GRAIN = 4
VMEM_LIMIT = 56 * 1024 * 1024


def gelu_cdf(value):
    return 0.5 + 0.5 * lax.erf(value * 0.7071067811865476)


def gelu_slope(value):
    density = jnp.exp(-0.5 * value * value) * 0.3989422804014327
    return gelu_cdf(value) + value * density


def tap_tables(quadrature, support, support_count, halo):
    kernel_count, rows, taps, slots = quadrature.shape
    bands = support.shape[0]
    band_rows = rows // bands
    live = lax.broadcasted_iota(jnp.int32, support.shape, 1) < support_count[:, None]
    lane = jnp.arange(LANES, dtype=jnp.int32)
    by_band = quadrature.reshape(kernel_count, bands, band_rows, taps, slots)

    def place(sign):
        hot = ((halo + sign * support)[:, :, None] == lane) & live[:, :, None]
        table = jnp.einsum(
            "kbrds,bsl->brkdl", by_band, hot.astype(jnp.bfloat16), preferred_element_type=jnp.float32
        )
        return table.reshape(rows, kernel_count, taps, LANES)

    row = jnp.arange(rows)[:, None, None, None]
    tap = jnp.arange(taps)[None, None, :, None]
    inside = (row + tap >= 1) & (row + tap <= rows)
    ahead = jnp.where(inside, place(1), 0.0)
    source = jnp.pad(place(-1), ((1, 1), (0, 0), (0, 0), (0, 0)))
    back = jnp.stack([source[e : e + rows, :, taps - 1 - e] for e in range(taps)], 2)
    shape = (rows, kernel_count * taps, LANES)
    return ahead.reshape(shape), back.reshape(shape)


def fill_matrices(table_ref, matrix_ref, row, cols):
    table = table_ref[row]
    for k in range(table.shape[0] // 3):
        for d in range(3):
            line = jnp.broadcast_to(table[k * 3 + d][None], (cols, LANES))
            rolled = pltpu.roll(line, 0, 1, stride=1, stride_axis=0)
            matrix_ref[row, k * cols : (k + 1) * cols, d * LANES : (d + 1) * LANES] = rolled.astype(
                jnp.bfloat16
            )


def spread_block(own, low, high, matrix, matrix_row, spread, first_row, count):
    rows, cols, channels = own.shape
    filler = jnp.zeros((LANES - cols - 2 * low.shape[1], channels), jnp.bfloat16)
    for r in range(count):
        parts = []
        for d in range(3):
            src = jnp.clip(first_row + r + d - 1, 0, rows - 1)
            parts += [low[src], own[src], high[src], filler]
        mixed = jnp.dot(
            matrix[matrix_row + r],
            jnp.concatenate(parts, 0),
            preferred_element_type=jnp.float32,
        ).astype(jnp.bfloat16)
        for k in range(mixed.shape[0] // cols):
            spread[r * cols : (r + 1) * cols, k * channels : (k + 1) * channels] = mixed[
                k * cols : (k + 1) * cols
            ]


def greet(partners):
    barrier = pltpu.get_barrier_semaphore()
    for other in partners:
        pl.semaphore_signal(
            barrier, inc=1, device_id={"lon": other}, device_id_type=pl.DeviceIdType.MESH
        )
    pl.semaphore_wait(barrier, len(partners))


def send(src, dst, send_sem, recv_sem, other):
    return pltpu.make_async_remote_copy(
        src_ref=src,
        dst_ref=dst,
        send_sem=send_sem,
        recv_sem=recv_sem,
        device_id={"lon": other},
        device_id_type=pl.DeviceIdType.MESH,
    )


def sides(size):
    me = lax.axis_index("lon")
    return [lax.rem(me + 1, size), lax.rem(me + size - 1, size)]


def edge_widths(rows, bands, widest):
    reach = [widest * (i // (rows // bands) + 1) // bands for i in range(rows)]
    return [-(-max(reach[max(i - 1, 0) : i + 2]) // GRAIN) * GRAIN for i in range(rows)]


def pack_edges(widths, field, to_right, to_left):
    cols = field.shape[1]
    begin, size, right, left = 0, 0, [], []
    for i, width in enumerate(widths):
        row = field[i]
        right.append(row[cols - width :])
        left.append(row[:width])
        size += width
        if i == len(widths) - 1 and size % 16:
            blank = jnp.zeros((-size % 16, field.shape[2]), field.dtype)
            right.append(blank)
            left.append(blank)
            size += blank.shape[0]
        if size % 16 == 0:
            to_right[begin : begin + size] = jnp.concatenate(right, 0)
            to_left[begin : begin + size] = jnp.concatenate(left, 0)
            begin, size, right, left = begin + size, 0, [], []


def unpack_edges(widths, edges, low, high):
    halo, channels = low.shape[1:]
    start = 0
    for i, width in enumerate(widths):
        first, last = start // 16 * 16, -(-(start + width) // 16) * 16
        cut = slice(start - first, start - first + width)
        below, above = edges[0][first:last][cut], edges[1][first:last][cut]
        blank = jnp.zeros((halo - width, channels), low.dtype)
        low[i] = jnp.concatenate([blank, below], 0)
        high[i] = jnp.concatenate([above, blank], 0)
        start += width


def edge_copies(size, to_right, to_left, edges, sems):
    right, left = sides(size)
    return [
        send(to_right, edges[0], sems.at[0], sems.at[1], right),
        send(to_left, edges[1], sems.at[2], sems.at[3], left),
    ]


def with_edges(size, widths, body, at_field, at_edges, *refs):
    *refs, to_right, to_left, sems = refs
    field, edges = refs[at_field], refs[at_edges : at_edges + 2]
    step = pl.program_id(0)

    @pl.when(step == 0)
    def _():
        pack_edges(widths, field, to_right, to_left)
        greet(sides(size))
        for copy in edge_copies(size, to_right, to_left, edges, sems):
            copy.start()

    body(*refs[:at_field], *refs[at_field + 1 : at_edges], *refs[at_edges + 2 :])

    @pl.when(step == pl.num_programs(0) - 1)
    def _():
        for copy in edge_copies(size, to_right, to_left, edges, sems):
            copy.wait()


def partners_of(size):
    me = lax.axis_index("lon")
    bit0, bit1 = lax.rem(me, 2), lax.rem(me // 2, 2)
    return [me + 1 - 2 * bit0, me + 2 - 4 * bit1] + [
        lax.rem(me + 4 * t, size) for t in range(1, size // 4)
    ]


def sum_stages(size, local, buffers, total, sems):
    got_half, half, got_quarter, quarter, got_piece, full = buffers
    me = lax.axis_index("lon")
    bit0, bit1, rank = lax.rem(me, 2), lax.rem(me // 2, 2), me // 4
    group = size // 4
    rows = local.shape[0]
    r2, r4, rp = rows // 2, rows // 4, rows // size
    others = partners_of(size)
    part = lambda ref, start, count: ref.at[pl.ds(pl.multiple_of(start, 16), count)]
    f32 = jnp.float32
    base0 = bit0 * r2
    base1 = base0 + bit1 * r4
    base2 = base1 + rank * rp
    pair = lambda i: (sems.at[2 * i], sems.at[2 * i + 1])

    halves = [send(part(local, (1 - bit0) * r2, r2), got_half, *pair(0), others[0])]
    quarters = [send(part(half, (1 - bit1) * r4, r4), got_quarter, *pair(1), others[1])]
    pieces, spreads = [], []
    for t in range(1, group):
        target = lax.rem(rank + t, group)
        pieces.append(
            send(part(quarter, target * rp, rp), got_piece.at[t - 1], *pair(3 + t), others[1 + t])
        )
        mine = part(full, base2, rp)
        spreads.append(send(mine, mine, *pair(2 + group + t), others[1 + t]))
    mine1, mine0 = part(full, base1, r4), part(full, base0, r2)
    back1 = [send(mine1, mine1, *pair(2), others[1])]
    back0 = [send(mine0, mine0, *pair(3), others[0])]

    def add_half():
        half[...] = (part(local, base0, r2)[...].astype(f32) + got_half[...].astype(f32)).astype(
            jnp.bfloat16
        )

    def add_quarter():
        quarter[...] = (
            part(half, bit1 * r4, r4)[...].astype(f32) + got_quarter[...].astype(f32)
        ).astype(jnp.bfloat16)

    def add_pieces():
        acc = part(quarter, rank * rp, rp)[...].astype(f32)
        for t in range(group - 1):
            acc = acc + got_piece[t].astype(f32)
        full[pl.ds(pl.multiple_of(base2, 16), rp), :] = acc.astype(jnp.bfloat16)

    def finish():
        total[...] = full[...].astype(f32)

    waits = [[], halves, quarters, pieces, spreads, back1, back0]
    works = [None, add_half, add_quarter, add_pieces, None, None, finish]
    starts = [halves, quarters, pieces, spreads, back1, back0, []]

    def stage(number):
        def run():
            for copy in waits[number]:
                copy.wait()
            if works[number] is not None:
                works[number]()
            for copy in starts[number]:
                copy.start()

        return run

    return [stage(number) for number in range(7)]


def sum_scratch(rows, channels, size):
    dims = [(rows // 2,), (rows // 2,), (rows // 4,), (rows // 4,), (size // 4 - 1, rows // size), (rows,)]
    return [pltpu.VMEM(dim + (channels,), jnp.bfloat16) for dim in dims] + [
        pltpu.SemaphoreType.DMA((2 * (2 + 2 * (size // 4)),))
    ]


SUM_STEPS = (1, 3, 5, 6, 7)


def run_stages(stages, step):
    for number, when in enumerate(SUM_STEPS, 1):

        @pl.when(step == when)
        def _():
            for chain in stages:
                chain[number]()


def matrices_kernel(block, cols, ahead_ref, back_ref, ahead_out, back_out):
    def body(row, carry):
        fill_matrices(ahead_ref, ahead_out, row, cols)
        fill_matrices(back_ref, back_out, row, cols)
        return carry

    lax.fori_loop(0, block, body, 0)


def add_outer(left, spread, grad_ref, step):
    part = lax.dot_general(
        left, spread, (((0,), (0,)), ((), ())), preferred_element_type=jnp.float32
    )

    @pl.when(step == 0)
    def _():
        grad_ref[...] = part

    @pl.when(step > 0)
    def _():
        grad_ref[...] += part


def first_kernel(widths, block, own, e0, e1, matrix, weight, pre_out, act_out, spread_out, low, high):
    step = pl.program_id(0)
    pl.when(step == 0)(lambda: unpack_edges(widths, (e0, e1), low, high))
    spread_block(own, low, high, matrix, 0, spread_out, step * block, block)
    pre = jnp.dot(spread_out[...], weight[...], preferred_element_type=jnp.float32)
    pre_out[...] = pre
    act_out[...] = (pre * gelu_cdf(pre)).astype(jnp.bfloat16).reshape(act_out.shape)


def slope_kernel(
    widths, block, scale, own, e0, e1, matrix, weight, pre, spread_one, gp_out, grad_out,
    low, high, spread, grad,
):
    step = pl.program_id(0)
    pl.when(step == 0)(lambda: unpack_edges(widths, (e0, e1), low, high))
    spread_block(own, low, high, matrix, 0, spread, step * block, block)
    grad_act = jnp.dot(spread[...], weight[...], preferred_element_type=jnp.float32)
    gp = (grad_act * gelu_slope(pre[...])).astype(jnp.bfloat16)
    gp_out[...] = gp.reshape(gp_out.shape)
    add_outer(gp, spread_one[...], grad, step)

    @pl.when(step == pl.num_programs(0) - 1)
    def _():
        grad_out[...] = (grad[...] * scale).T.astype(jnp.bfloat16)


def second_kernel(
    widths, block, scale, own, e0, e1, matrix, weight, resid, cot, mixed_out, grad_out,
    low, high, spread, grad,
):
    step = pl.program_id(0)
    pl.when(step == 0)(lambda: unpack_edges(widths, (e0, e1), low, high))
    spread_block(own, low, high, matrix, 0, spread, step * block, block)
    branch = jnp.dot(spread[...], weight[...], preferred_element_type=jnp.float32)
    flat = branch.shape
    mixed_out[...] = (
        (resid[...].reshape(flat).astype(jnp.float32) + branch)
        .astype(jnp.bfloat16)
        .reshape(mixed_out.shape)
    )
    add_outer(cot[...].reshape(flat), spread[...], grad, step)

    @pl.when(step == pl.num_programs(0) - 1)
    def _():
        grad_out[...] = (grad[...] * scale).T.astype(jnp.bfloat16)


def last_kernel(
    size, widths, block, own, e0, e1, matrix, weight, cot, grad_first, grad_second,
    field_out, total_first, total_second, low, high, spread, *work
):
    step = pl.program_id(0)
    half = len(work) // 2
    stages = [
        sum_stages(size, grad_first, work[: half - 1], total_first, work[half - 1]),
        sum_stages(size, grad_second, work[half:-1], total_second, work[-1]),
    ]

    @pl.when(step == 0)
    def _():
        greet(partners_of(size))
        for chain in stages:
            chain[0]()
        unpack_edges(widths, (e0, e1), low, high)

    run_stages(stages, step)
    spread_block(own, low, high, matrix, 0, spread, step * block, block)
    adj = jnp.dot(spread[...], weight[...], preferred_element_type=jnp.float32)
    field_out[...] = (
        (cot[...].reshape(adj.shape).astype(jnp.float32) + adj)
        .astype(jnp.bfloat16)
        .reshape(field_out.shape)
    )

    @pl.when(step == pl.num_programs(0) - 1)
    def _():
        for chain in stages:
            chain[-1]()


def on_device(
    activations, quadrature, support, support_count, weight_first, weight_second, cotangent
):
    rows, cols, channels = activations.shape
    kernels = weight_first.shape[0]
    halo = -(-(cols // 2) // 16) * 16
    block = 8
    steps = rows // block
    wide = kernels * channels
    scale = 1.0 / math.sqrt(rows * cols * lax.axis_size("lon"))
    flat_first = weight_first.reshape(wide, channels)
    flat_second = weight_second.reshape(wide, channels)
    turned_first = weight_first.swapaxes(1, 2).reshape(wide, channels)
    turned_second = weight_second.swapaxes(1, 2).reshape(wide, channels)
    ahead, back = tap_tables(quadrature, support, support_count, halo)

    bf16, f32 = jnp.bfloat16, jnp.float32
    whole = lambda shape: pl.BlockSpec(shape, lambda i: (0,) * len(shape))
    by_row = lambda shape: pl.BlockSpec(shape, lambda i: (i,) + (0,) * (len(shape) - 1))
    field_spec = by_row((block, cols, channels))
    matrix_spec = by_row((block, kernels * cols, 3 * LANES))
    bands = support.shape[0]
    widths = edge_widths(rows, bands, cols // 2)
    edge_shapes = [(-(-sum(widths) // 16) * 16, channels)] * 2
    common = (
        [whole((rows, cols, channels))]
        + [whole(shape) for shape in edge_shapes]
        + [matrix_spec, whole((wide, channels))]
    )
    spread_shape = (block * cols, wide)
    field_type = jax.ShapeDtypeStruct((rows, cols, channels), bf16)
    grad_type = jax.ShapeDtypeStruct((wide, channels), bf16)
    work = [pltpu.VMEM(spread_shape, bf16), pltpu.VMEM((channels, wide), f32)]
    size = lax.axis_size("lon")
    assert steps == 8 and size % 4 == 0

    def call(number, body, **kw):
        return pl.pallas_call(
            body,
            grid=(steps,),
            compiler_params=pltpu.CompilerParams(
                vmem_limit_bytes=VMEM_LIMIT, collective_id=number, has_side_effects=True
            ),
            **kw,
        )

    matrix_type = jax.ShapeDtypeStruct((rows, kernels * cols, 3 * LANES), bf16)
    edge_types = [jax.ShapeDtypeStruct(shape, bf16) for shape in edge_shapes]
    field_whole = whole((rows, cols, channels))
    unpacked = [pltpu.VMEM((rows, halo, channels), bf16)] * 2
    total_type = jax.ShapeDtypeStruct((wide, channels), f32)
    anywhere = pl.BlockSpec(memory_space=pl.ANY)
    edge_work = [pltpu.VMEM(shape, bf16) for shape in edge_shapes] + [pltpu.SemaphoreType.DMA((4,))]
    table_spec = by_row((block, kernels * 3, LANES))
    edged = lambda body, at_field, at_edges: functools.partial(
        with_edges, size, widths, body, at_field, at_edges
    )
    m_ahead, m_back, *act_edges = call(
        0,
        edged(functools.partial(matrices_kernel, block, cols), 2, 5),
        in_specs=[table_spec, table_spec, field_whole],
        out_specs=[matrix_spec, matrix_spec] + [anywhere] * 2,
        out_shape=[matrix_type, matrix_type] + edge_types,
        scratch_shapes=edge_work,
    )(ahead, back, activations)
    cells = rows * cols
    pre, activated, spread_one, *cot_edges = call(
        1,
        edged(functools.partial(first_kernel, widths, block), 5, 9),
        in_specs=common + [field_whole],
        out_specs=[by_row((block * cols, channels)), field_spec, by_row(spread_shape)]
        + [anywhere] * 2,
        out_shape=[
            jax.ShapeDtypeStruct((cells, channels), f32),
            field_type,
            jax.ShapeDtypeStruct((cells, wide), bf16),
        ]
        + edge_types,
        scratch_shapes=unpacked + edge_work,
    )(activations, *act_edges, m_ahead, flat_first, cotangent)
    gp, grad_first, *mid_edges = call(
        2,
        edged(functools.partial(slope_kernel, widths, block, scale), 7, 10),
        in_specs=common + [by_row((block * cols, channels)), by_row(spread_shape), field_whole],
        out_specs=[field_spec, whole((wide, channels))] + [anywhere] * 2,
        out_shape=[field_type, grad_type] + edge_types,
        scratch_shapes=unpacked + work + edge_work,
    )(cotangent, *cot_edges, m_back, turned_second, pre, spread_one, activated)
    mixed, grad_second, *gp_edges = call(
        3,
        edged(functools.partial(second_kernel, widths, block, scale), 7, 10),
        in_specs=common + [field_spec, field_spec, field_whole],
        out_specs=[field_spec, whole((wide, channels))] + [anywhere] * 2,
        out_shape=[field_type, grad_type] + edge_types,
        scratch_shapes=unpacked + work + edge_work,
    )(activated, *mid_edges, m_ahead, flat_second, activations, cotangent, gp)
    grad_spec = whole((wide, channels))
    grad_field, total_first, total_second = call(
        4,
        functools.partial(last_kernel, size, widths, block),
        in_specs=common + [field_spec, grad_spec, grad_spec],
        out_specs=[field_spec, grad_spec, grad_spec],
        out_shape=[field_type, total_type, total_type],
        scratch_shapes=unpacked
        + work[:1]
        + sum_scratch(wide, channels, size) * 2,
    )(gp, *gp_edges, m_back, turned_first, cotangent, grad_first, grad_second)
    return (
        mixed,
        grad_field,
        total_first.reshape(kernels, channels, channels),
        total_second.reshape(kernels, channels, channels),
    )


def solution(mesh):
    placed = (P("ens", "lon", None), P(), P(), P(), P(), P(), P("ens", "lon", None))
    return jax.shard_map(
        on_device,
        mesh=mesh,
        in_specs=placed,
        out_specs=(
            P("ens", "lon", None),
            P("ens", "lon", None),
            P("ens", None, None),
            P("ens", None, None),
        ),
        check_vma=False,
    )
```

```python
import functools
import math

import jax
import jax.numpy as jnp
from jax import lax
from jax.experimental import pallas as pl
from jax.experimental.pallas import tpu as pltpu
from jax.sharding import PartitionSpec as P

LANES = 128
GRAIN = 2
VMEM_LIMIT = 56 * 1024 * 1024


def gelu_cdf(value):
    return 0.5 + 0.5 * lax.erf(value * 0.7071067811865476)


def gelu_slope(value):
    density = jnp.exp(-0.5 * value * value) * 0.3989422804014327
    return gelu_cdf(value) + value * density


def tap_tables(quadrature, support, support_count, halo):
    kernel_count, rows, taps, slots = quadrature.shape
    bands = support.shape[0]
    band_rows = rows // bands
    live = lax.broadcasted_iota(jnp.int32, support.shape, 1) < support_count[:, None]
    lane = jnp.arange(LANES, dtype=jnp.int32)
    by_band = quadrature.reshape(kernel_count, bands, band_rows, taps, slots)

    def place(sign):
        hot = ((halo + sign * support)[:, :, None] == lane) & live[:, :, None]
        table = jnp.einsum(
            "kbrds,bsl->brkdl", by_band, hot.astype(jnp.bfloat16), preferred_element_type=jnp.float32
        )
        return table.reshape(rows, kernel_count, taps, LANES)

    row = jnp.arange(rows)[:, None, None, None]
    tap = jnp.arange(taps)[None, None, :, None]
    inside = (row + tap >= 1) & (row + tap <= rows)
    ahead = jnp.where(inside, place(1), 0.0)
    source = jnp.pad(place(-1), ((1, 1), (0, 0), (0, 0), (0, 0)))
    back = jnp.stack([source[e : e + rows, :, taps - 1 - e] for e in range(taps)], 2)
    shape = (rows, kernel_count * taps, LANES)
    return ahead.reshape(shape), back.reshape(shape)


def fill_matrices(table_ref, matrix_ref, row, cols):
    table = table_ref[row]
    for k in range(table.shape[0] // 3):
        for d in range(3):
            line = jnp.broadcast_to(table[k * 3 + d][None], (cols, LANES))
            rolled = pltpu.roll(line, 0, 1, stride=1, stride_axis=0)
            matrix_ref[row, k * cols : (k + 1) * cols, d * LANES : (d + 1) * LANES] = rolled.astype(
                jnp.bfloat16
            )


def spread_block(own, low, high, matrix, matrix_row, spread, first_row, count):
    rows, cols, channels = own.shape
    filler = jnp.zeros((LANES - cols - 2 * low.shape[1], channels), jnp.bfloat16)
    for r in range(count):
        parts = []
        for d in range(3):
            src = jnp.clip(first_row + r + d - 1, 0, rows - 1)
            parts += [low[src], own[src], high[src], filler]
        mixed = jnp.dot(
            matrix[matrix_row + r],
            jnp.concatenate(parts, 0),
            preferred_element_type=jnp.float32,
        ).astype(jnp.bfloat16)
        for k in range(mixed.shape[0] // cols):
            spread[r * cols : (r + 1) * cols, k * channels : (k + 1) * channels] = mixed[
                k * cols : (k + 1) * cols
            ]


def greet(partners):
    barrier = pltpu.get_barrier_semaphore()
    for other in partners:
        pl.semaphore_signal(
            barrier, inc=1, device_id={"lon": other}, device_id_type=pl.DeviceIdType.MESH
        )
    pl.semaphore_wait(barrier, len(partners))


def send(src, dst, send_sem, recv_sem, other):
    return pltpu.make_async_remote_copy(
        src_ref=src,
        dst_ref=dst,
        send_sem=send_sem,
        recv_sem=recv_sem,
        device_id={"lon": other},
        device_id_type=pl.DeviceIdType.MESH,
    )


def sides(size):
    me = lax.axis_index("lon")
    return [lax.rem(me + 1, size), lax.rem(me + size - 1, size)]


def edge_widths(rows, bands, widest):
    reach = [widest * (i // (rows // bands) + 1) // bands for i in range(rows)]
    return [-(-max(reach[max(i - 1, 0) : i + 2]) // GRAIN) * GRAIN for i in range(rows)]


def pack_edges(widths, field, to_right, to_left):
    cols = field.shape[1]
    begin, size, right, left = 0, 0, [], []
    for i, width in enumerate(widths):
        row = field[i]
        right.append(row[cols - width :])
        left.append(row[:width])
        size += width
        if i == len(widths) - 1 and size % 16:
            blank = jnp.zeros((-size % 16, field.shape[2]), field.dtype)
            right.append(blank)
            left.append(blank)
            size += blank.shape[0]
        if size % 16 == 0:
            to_right[begin : begin + size] = jnp.concatenate(right, 0)
            to_left[begin : begin + size] = jnp.concatenate(left, 0)
            begin, size, right, left = begin + size, 0, [], []


def unpack_edges(widths, edges, low, high):
    halo, channels = low.shape[1:]
    start = 0
    for i, width in enumerate(widths):
        first, last = start // 16 * 16, -(-(start + width) // 16) * 16
        cut = slice(start - first, start - first + width)
        below, above = edges[0][first:last][cut], edges[1][first:last][cut]
        blank = jnp.zeros((halo - width, channels), low.dtype)
        low[i] = jnp.concatenate([blank, below], 0)
        high[i] = jnp.concatenate([above, blank], 0)
        start += width


def edge_copies(size, to_right, to_left, edges, sems):
    right, left = sides(size)
    return [
        send(to_right, edges[0], sems.at[0], sems.at[1], right),
        send(to_left, edges[1], sems.at[2], sems.at[3], left),
    ]


def with_edges(size, widths, body, at_field, at_edges, *refs):
    *refs, to_right, to_left, sems = refs
    field, edges = refs[at_field], refs[at_edges : at_edges + 2]
    step = pl.program_id(0)

    @pl.when(step == 0)
    def _():
        pack_edges(widths, field, to_right, to_left)
        greet(sides(size))
        for copy in edge_copies(size, to_right, to_left, edges, sems):
            copy.start()

    body(*refs[:at_field], *refs[at_field + 1 : at_edges], *refs[at_edges + 2 :])

    @pl.when(step == pl.num_programs(0) - 1)
    def _():
        for copy in edge_copies(size, to_right, to_left, edges, sems):
            copy.wait()


def partners_of(size):
    me = lax.axis_index("lon")
    bit0, bit1 = lax.rem(me, 2), lax.rem(me // 2, 2)
    return [me + 1 - 2 * bit0, me + 2 - 4 * bit1] + [
        lax.rem(me + 4 * t, size) for t in range(1, size // 4)
    ]


def sum_stages(size, local, buffers, total, sems):
    got_half, half, got_quarter, quarter, got_piece, full = buffers
    me = lax.axis_index("lon")
    bit0, bit1, rank = lax.rem(me, 2), lax.rem(me // 2, 2), me // 4
    group = size // 4
    rows = local.shape[0]
    r2, r4, rp = rows // 2, rows // 4, rows // size
    others = partners_of(size)
    part = lambda ref, start, count: ref.at[pl.ds(pl.multiple_of(start, 16), count)]
    f32 = jnp.float32
    base0 = bit0 * r2
    base1 = base0 + bit1 * r4
    base2 = base1 + rank * rp
    pair = lambda i: (sems.at[2 * i], sems.at[2 * i + 1])

    halves = [send(part(local, (1 - bit0) * r2, r2), got_half, *pair(0), others[0])]
    quarters = [send(part(half, (1 - bit1) * r4, r4), got_quarter, *pair(1), others[1])]
    pieces, spreads = [], []
    for t in range(1, group):
        target = lax.rem(rank + t, group)
        pieces.append(
            send(part(quarter, target * rp, rp), got_piece.at[t - 1], *pair(3 + t), others[1 + t])
        )
        mine = part(full, base2, rp)
        spreads.append(send(mine, mine, *pair(2 + group + t), others[1 + t]))
    mine1, mine0 = part(full, base1, r4), part(full, base0, r2)
    back1 = [send(mine1, mine1, *pair(2), others[1])]
    back0 = [send(mine0, mine0, *pair(3), others[0])]

    def add_half():
        half[...] = (part(local, base0, r2)[...].astype(f32) + got_half[...].astype(f32)).astype(
            jnp.bfloat16
        )

    def add_quarter():
        quarter[...] = (
            part(half, bit1 * r4, r4)[...].astype(f32) + got_quarter[...].astype(f32)
        ).astype(jnp.bfloat16)

    def add_pieces():
        acc = part(quarter, rank * rp, rp)[...].astype(f32)
        for t in range(group - 1):
            acc = acc + got_piece[t].astype(f32)
        full[pl.ds(pl.multiple_of(base2, 16), rp), :] = acc.astype(jnp.bfloat16)

    def finish():
        total[...] = full[...].astype(f32)

    waits = [[], halves, quarters, pieces, spreads, back1, back0]
    works = [None, add_half, add_quarter, add_pieces, None, None, finish]
    starts = [halves, quarters, pieces, spreads, back1, back0, []]

    def stage(number):
        def run():
            for copy in waits[number]:
                copy.wait()
            if works[number] is not None:
                works[number]()
            for copy in starts[number]:
                copy.start()

        return run

    return [stage(number) for number in range(7)]


def sum_scratch(rows, channels, size):
    dims = [(rows // 2,), (rows // 2,), (rows // 4,), (rows // 4,), (size // 4 - 1, rows // size), (rows,)]
    return [pltpu.VMEM(dim + (channels,), jnp.bfloat16) for dim in dims] + [
        pltpu.SemaphoreType.DMA((2 * (2 + 2 * (size // 4)),))
    ]


SUM_STEPS = (1, 3, 5, 6, 7)


def run_stages(stages, step):
    for number, when in enumerate(SUM_STEPS, 1):

        @pl.when(step == when)
        def _():
            for chain in stages:
                chain[number]()


def matrices_kernel(block, cols, ahead_ref, back_ref, ahead_out, back_out):
    def body(row, carry):
        fill_matrices(ahead_ref, ahead_out, row, cols)
        fill_matrices(back_ref, back_out, row, cols)
        return carry

    lax.fori_loop(0, block, body, 0)


def add_outer(left, spread, grad_ref, step):
    part = lax.dot_general(
        left, spread, (((0,), (0,)), ((), ())), preferred_element_type=jnp.float32
    )

    @pl.when(step == 0)
    def _():
        grad_ref[...] = part

    @pl.when(step > 0)
    def _():
        grad_ref[...] += part


def first_kernel(widths, block, own, e0, e1, matrix, weight, pre_out, act_out, spread_out, low, high):
    step = pl.program_id(0)
    pl.when(step == 0)(lambda: unpack_edges(widths, (e0, e1), low, high))
    spread_block(own, low, high, matrix, 0, spread_out, step * block, block)
    pre = jnp.dot(spread_out[...], weight[...], preferred_element_type=jnp.float32)
    pre_out[...] = pre
    act_out[...] = (pre * gelu_cdf(pre)).astype(jnp.bfloat16).reshape(act_out.shape)


def slope_kernel(
    widths, block, scale, own, e0, e1, matrix, weight, pre, spread_one, gp_out, grad_out,
    low, high, spread, grad,
):
    step = pl.program_id(0)
    pl.when(step == 0)(lambda: unpack_edges(widths, (e0, e1), low, high))
    spread_block(own, low, high, matrix, 0, spread, step * block, block)
    grad_act = jnp.dot(spread[...], weight[...], preferred_element_type=jnp.float32)
    gp = (grad_act * gelu_slope(pre[...])).astype(jnp.bfloat16)
    gp_out[...] = gp.reshape(gp_out.shape)
    add_outer(gp, spread_one[...], grad, step)

    @pl.when(step == pl.num_programs(0) - 1)
    def _():
        grad_out[...] = (grad[...] * scale).T.astype(jnp.bfloat16)


def second_kernel(
    widths, block, scale, own, e0, e1, matrix, weight, resid, cot, mixed_out, grad_out,
    low, high, spread, grad,
):
    step = pl.program_id(0)
    pl.when(step == 0)(lambda: unpack_edges(widths, (e0, e1), low, high))
    spread_block(own, low, high, matrix, 0, spread, step * block, block)
    branch = jnp.dot(spread[...], weight[...], preferred_element_type=jnp.float32)
    flat = branch.shape
    mixed_out[...] = (
        (resid[...].reshape(flat).astype(jnp.float32) + branch)
        .astype(jnp.bfloat16)
        .reshape(mixed_out.shape)
    )
    add_outer(cot[...].reshape(flat), spread[...], grad, step)

    @pl.when(step == pl.num_programs(0) - 1)
    def _():
        grad_out[...] = (grad[...] * scale).T.astype(jnp.bfloat16)


def last_kernel(
    size, widths, block, own, e0, e1, matrix, weight, cot, grad_first, grad_second,
    field_out, total_first, total_second, low, high, spread, *work
):
    step = pl.program_id(0)
    each, rows = len(work) // 4, grad_first.shape[0] // 2
    stages = []
    for number in range(4):
        cut = pl.ds(number // 2 * rows, rows)
        grad, total = ((grad_first, total_first), (grad_second, total_second))[number % 2]
        *buffers, sems = work[number * each : (number + 1) * each]
        stages.append(sum_stages(size, grad.at[cut], buffers, total.at[cut], sems))

    @pl.when(step == 0)
    def _():
        greet(partners_of(size))
        for chain in stages:
            chain[0]()
        unpack_edges(widths, (e0, e1), low, high)

    run_stages(stages, step)
    spread_block(own, low, high, matrix, 0, spread, step * block, block)
    adj = jnp.dot(spread[...], weight[...], preferred_element_type=jnp.float32)
    field_out[...] = (
        (cot[...].reshape(adj.shape).astype(jnp.float32) + adj)
        .astype(jnp.bfloat16)
        .reshape(field_out.shape)
    )

    @pl.when(step == pl.num_programs(0) - 1)
    def _():
        for chain in stages:
            chain[-1]()


def on_device(
    activations, quadrature, support, support_count, weight_first, weight_second, cotangent
):
    rows, cols, channels = activations.shape
    kernels = weight_first.shape[0]
    halo = -(-(cols // 2) // 16) * 16
    block = 8
    steps = rows // block
    wide = kernels * channels
    scale = 1.0 / math.sqrt(rows * cols * lax.axis_size("lon"))
    flat_first = weight_first.reshape(wide, channels)
    flat_second = weight_second.reshape(wide, channels)
    turned_first = weight_first.swapaxes(1, 2).reshape(wide, channels)
    turned_second = weight_second.swapaxes(1, 2).reshape(wide, channels)
    ahead, back = tap_tables(quadrature, support, support_count, halo)

    bf16, f32 = jnp.bfloat16, jnp.float32
    whole = lambda shape: pl.BlockSpec(shape, lambda i: (0,) * len(shape))
    by_row = lambda shape: pl.BlockSpec(shape, lambda i: (i,) + (0,) * (len(shape) - 1))
    field_spec = by_row((block, cols, channels))
    matrix_spec = by_row((block, kernels * cols, 3 * LANES))
    bands = support.shape[0]
    widths = edge_widths(rows, bands, cols // 2)
    edge_shapes = [(-(-sum(widths) // 16) * 16, channels)] * 2
    common = (
        [whole((rows, cols, channels))]
        + [whole(shape) for shape in edge_shapes]
        + [matrix_spec, whole((wide, channels))]
    )
    spread_shape = (block * cols, wide)
    field_type = jax.ShapeDtypeStruct((rows, cols, channels), bf16)
    grad_type = jax.ShapeDtypeStruct((wide, channels), bf16)
    work = [pltpu.VMEM(spread_shape, bf16), pltpu.VMEM((channels, wide), f32)]
    size = lax.axis_size("lon")
    assert steps == 8 and size % 4 == 0

    def call(number, body, **kw):
        return pl.pallas_call(
            body,
            grid=(steps,),
            compiler_params=pltpu.CompilerParams(
                vmem_limit_bytes=VMEM_LIMIT, collective_id=number, has_side_effects=True
            ),
            **kw,
        )

    matrix_type = jax.ShapeDtypeStruct((rows, kernels * cols, 3 * LANES), bf16)
    edge_types = [jax.ShapeDtypeStruct(shape, bf16) for shape in edge_shapes]
    field_whole = whole((rows, cols, channels))
    unpacked = [pltpu.VMEM((rows, halo, channels), bf16)] * 2
    total_type = jax.ShapeDtypeStruct((wide, channels), f32)
    anywhere = pl.BlockSpec(memory_space=pl.ANY)
    edge_work = [pltpu.VMEM(shape, bf16) for shape in edge_shapes] + [pltpu.SemaphoreType.DMA((4,))]
    table_spec = by_row((block, kernels * 3, LANES))
    edged = lambda body, at_field, at_edges: functools.partial(
        with_edges, size, widths, body, at_field, at_edges
    )
    m_ahead, m_back, *act_edges = call(
        0,
        edged(functools.partial(matrices_kernel, block, cols), 2, 5),
        in_specs=[table_spec, table_spec, field_whole],
        out_specs=[matrix_spec, matrix_spec] + [anywhere] * 2,
        out_shape=[matrix_type, matrix_type] + edge_types,
        scratch_shapes=edge_work,
    )(ahead, back, activations)
    cells = rows * cols
    pre, activated, spread_one, *cot_edges = call(
        1,
        edged(functools.partial(first_kernel, widths, block), 5, 9),
        in_specs=common + [field_whole],
        out_specs=[by_row((block * cols, channels)), field_spec, by_row(spread_shape)]
        + [anywhere] * 2,
        out_shape=[
            jax.ShapeDtypeStruct((cells, channels), f32),
            field_type,
            jax.ShapeDtypeStruct((cells, wide), bf16),
        ]
        + edge_types,
        scratch_shapes=unpacked + edge_work,
    )(activations, *act_edges, m_ahead, flat_first, cotangent)
    gp, grad_first, *mid_edges = call(
        2,
        edged(functools.partial(slope_kernel, widths, block, scale), 7, 10),
        in_specs=common + [by_row((block * cols, channels)), by_row(spread_shape), field_whole],
        out_specs=[field_spec, whole((wide, channels))] + [anywhere] * 2,
        out_shape=[field_type, grad_type] + edge_types,
        scratch_shapes=unpacked + work + edge_work,
    )(cotangent, *cot_edges, m_back, turned_second, pre, spread_one, activated)
    mixed, grad_second, *gp_edges = call(
        3,
        edged(functools.partial(second_kernel, widths, block, scale), 7, 10),
        in_specs=common + [field_spec, field_spec, field_whole],
        out_specs=[field_spec, whole((wide, channels))] + [anywhere] * 2,
        out_shape=[field_type, grad_type] + edge_types,
        scratch_shapes=unpacked + work + edge_work,
    )(activated, *mid_edges, m_ahead, flat_second, activations, cotangent, gp)
    grad_spec = whole((wide, channels))
    grad_field, total_first, total_second = call(
        4,
        functools.partial(last_kernel, size, widths, block),
        in_specs=common + [field_spec, grad_spec, grad_spec],
        out_specs=[field_spec, grad_spec, grad_spec],
        out_shape=[field_type, total_type, total_type],
        scratch_shapes=unpacked
        + work[:1]
        + sum_scratch(wide // 2, channels, size) * 4,
    )(gp, *gp_edges, m_back, turned_first, cotangent, grad_first, grad_second)
    return (
        mixed,
        grad_field,
        total_first.reshape(kernels, channels, channels),
        total_second.reshape(kernels, channels, channels),
    )


def solution(mesh):
    placed = (P("ens", "lon", None), P(), P(), P(), P(), P(), P("ens", "lon", None))
    return jax.shard_map(
        on_device,
        mesh=mesh,
        in_specs=placed,
        out_specs=(
            P("ens", "lon", None),
            P("ens", "lon", None),
            P("ens", None, None),
            P("ens", None, None),
        ),
        check_vma=False,
    )
```
